32 devices in a mesh: lat: 8 (over z, x), lon: 4 (over y, core).
Axes of the slice: x: 2, y: 2, z: 4, core: 2. Of those that a mesh axis runs over, the one named last changes fastest.
Arguments:
- stream: bfloat16 [128, 1024, 256], P('lat', 'lon'), may hold values from -6 to 6
- cotangent: bfloat16 [128, 1024, 256], P('lat', 'lon'), may hold values from -6 to 6
- w_expand: bfloat16 [256, 512], replicated, may hold values from -0.375 to 0.375
- w_reduce: bfloat16 [512, 256], replicated, may hold values from -0.25 to 0.25
- legendre: bfloat16 [512, 128, 512], P(('lat', 'lon')), as said below
- quadrature: float32 [128], replicated, may hold values from 0.2 to 2
- spectral_mix: bfloat16 [512, 256, 256], P(('lat', 'lon')), may hold values from -0.375 to 0.375
Outputs:
- grad_input: bfloat16 [128, 1024, 256], P('lat', 'lon')
- grad_expand: float32 [256, 512], replicated
- grad_reduce: float32 [512, 256], replicated
The draws below stay inside these ranges and needn't reach their ends.
Inputs may be any that keep to these rules, and one draw needn't show every extreme that they name: legendre[m, a, l] is zero wherever l < m.
All inputs are finite; a program needn't handle non-finite values.
Results may differ from the reference program's by a relative error of at most 0.009.
Values may be sent and summed in bfloat16 or wider, within the bound.
A program may use at most 128 MiB of HBM per device.

```python
import math
import jax
import jax.numpy as jnp
from jax import lax

C = 256
FFN = 512
NLON = 1024
LAT_DEV = 16
NLAT = 128
MM = 512
L = 512
TOKENS = 131072


def draw_legendre(key, part):
    values = jax.random.normal(key, (MM, NLAT, L), jnp.float32) * (1.0 / NLAT ** 0.5)
    values = jnp.clip(values, -6.0 / NLAT ** 0.5, 6.0 / NLAT ** 0.5)
    order_index = lax.broadcasted_iota(jnp.int32, (MM, NLAT, L), 0)
    degree_index = lax.broadcasted_iota(jnp.int32, (MM, NLAT, L), 2)
    kept = jnp.where(degree_index >= order_index, values, jnp.zeros_like(values))
    return kept.astype(jnp.bfloat16)


def steps_of(stream_key, extent, split, low, largest):
    gain = 1.0
    for dim, parts in split:
        steps = jax.random.uniform(jax.random.fold_in(jax.random.fold_in(stream_key, 6), dim), (parts,), jnp.float32, low / len(split), largest / len(split))
        gain = gain * jnp.repeat(jnp.exp(steps), extent[dim] // parts).reshape((-1,) + (1,) * (len(extent) - 1 - dim))
    return gain


def noise(rng, dims, deviation, reach, split=(), kind=jnp.bfloat16):
    entries = deviation * jax.random.normal(rng, dims, jnp.float32)
    if split:
        entries = entries * steps_of(rng, dims, split, -0.22, 0.18)
    return jnp.clip(entries, -reach, reach).astype(kind)


def setup_inputs(seed: int = 0) -> dict:
    key_of = jax.random.split(jax.random.key(seed), 8)
    return {
        "stream": noise(key_of[0], (NLAT, NLON, C), 1.0, 6.0, ((0, 8), (1, 4))),
        "cotangent": noise(key_of[1], (NLAT, NLON, C), 1.0, 6.0, ((0, 8), (1, 4))),
        "w_expand": noise(key_of[2], (C, FFN), C ** -0.5, 0.375),
        "w_reduce": noise(key_of[3], (FFN, C), FFN ** -0.5, 0.25),
        "legendre": draw_legendre(jax.random.fold_in(key_of[7], 71), 0),
        "quadrature": jnp.clip(jnp.exp(jax.random.uniform(key_of[5], (NLAT,), jnp.float32, math.log(0.2), math.log(2.0))), 0.2, 2.0),
        "spectral_mix": noise(key_of[6], (L, C, C), C ** -0.5, 0.375, ((0, 32),)),
    }


def gelu_value(preact):
    inside = 0.7978845608028654 * (preact + 0.044715 * preact * preact * preact)
    return 0.5 * preact * (1.0 + jnp.tanh(inside))

def gelu_slope(preact):
    inside = 0.7978845608028654 * (preact + 0.044715 * preact * preact * preact)
    tanh_val = jnp.tanh(inside)
    return 0.5 * (1.0 + tanh_val) + 0.5 * preact * (1.0 - tanh_val * tanh_val) * 0.7978845608028654 * (1.0 + 3.0 * 0.044715 * preact * preact)

def dft_table(count, order_count):
    lon_index = jnp.arange(count, dtype=jnp.int32)[:, None]
    order_index = jnp.arange(order_count, dtype=jnp.int32)[None, :]
    angles = (lon_index * order_index % count).astype(jnp.float32) * (2.0 * math.pi / count)
    factor = 1.0 / math.sqrt(count)
    return jnp.stack([jnp.cos(angles) * factor, -jnp.sin(angles) * factor]).astype(jnp.bfloat16)

def reference(stream, cotangent, w_expand, w_reduce, legendre, quadrature, spectral_mix):
    block_count = NLAT // LAT_DEV
    basis = dft_table(NLON, MM)
    basis_wide = basis.astype(jnp.float32)

    def front_pass(totals, pieces):
        rows_block, grad_block = pieces
        tokens = rows_block.reshape(-1, C)
        upstream = grad_block.reshape(-1, C)
        preact = jnp.dot(tokens, w_expand, preferred_element_type=jnp.float32)
        active = gelu_value(preact).astype(jnp.bfloat16)
        through = jnp.dot(upstream, w_reduce.T, preferred_element_type=jnp.float32)
        dpreact = (through * gelu_slope(preact)).astype(jnp.bfloat16)
        new_in = totals[0] + jnp.dot(tokens.T, dpreact, preferred_element_type=jnp.float32)
        new_out = totals[1] + jnp.dot(active.T, upstream, preferred_element_type=jnp.float32)
        skip_grad = (upstream.astype(jnp.float32) + jnp.dot(dpreact, w_expand.T, preferred_element_type=jnp.float32)).astype(jnp.bfloat16)
        skip_grad = skip_grad.reshape(LAT_DEV, NLON, C)
        fourier = jnp.einsum('anc,knm->kacm', skip_grad.astype(jnp.float32), basis_wide).astype(jnp.bfloat16)
        return ((new_in, new_out), (skip_grad, fourier))
    start = (jnp.zeros((C, FFN), jnp.float32), jnp.zeros((FFN, C), jnp.float32))
    pieces = (stream.reshape(block_count, LAT_DEV, NLON, C), cotangent.reshape(block_count, LAT_DEV, NLON, C))
    (grad_in, grad_out), (skip_grad, fourier) = lax.scan(front_pass, start, pieces)
    fourier = jnp.transpose(fourier, (4, 1, 0, 2, 3)).reshape(MM, 2, NLAT, C)
    mix_wide = spectral_mix.astype(jnp.float32)

    def per_order(pieces):
        table_order, coef_order = pieces
        legendre_wide = table_order.astype(jnp.float32)
        by_order = jnp.einsum('al,kac->klc', legendre_wide, coef_order.astype(jnp.float32)).astype(jnp.bfloat16)
        mixed_coef = jnp.einsum('klc,ldc->kld', by_order.astype(jnp.float32), mix_wide).astype(jnp.bfloat16)
        summed = jnp.einsum('al,kld->kad', legendre_wide, mixed_coef.astype(jnp.float32))
        return (summed * quadrature[None, :, None]).astype(jnp.bfloat16)
    synthesis = lax.map(per_order, (legendre, fourier))
    synthesis = jnp.transpose(synthesis.reshape(MM, 2, block_count, LAT_DEV, C), (2, 0, 1, 3, 4))

    def rear_pass(pieces):
        synth_block, skip_block = pieces
        grid_back = jnp.einsum('mkac,knm->anc', synth_block.astype(jnp.float32), basis_wide).astype(jnp.bfloat16)
        return (skip_block.astype(jnp.float32) + grid_back.astype(jnp.float32)).astype(jnp.bfloat16)
    grad_input = lax.map(rear_pass, (synthesis, skip_grad)).reshape(NLAT, NLON, C)
    factor = 1.0 / math.sqrt(TOKENS)
    return (grad_input, grad_in * factor, grad_out * factor)
```

```python
import functools
import math

import jax
import jax.numpy as jnp
from jax import lax
from jax.experimental import pallas as pl
from jax.experimental.pallas import tpu as pltpu
from jax.sharding import PartitionSpec as P


def gelu_value(preact):
    inside = 0.7978845608028654 * (preact + 0.044715 * preact * preact * preact)
    return 0.5 * preact * (1.0 + jnp.tanh(inside))


def gelu_slope(preact):
    inside = 0.7978845608028654 * (preact + 0.044715 * preact * preact * preact)
    tanh_val = jnp.tanh(inside)
    return 0.5 * (1.0 + tanh_val) + 0.5 * preact * (
        1.0 - tanh_val * tanh_val
    ) * 0.7978845608028654 * (1.0 + 3.0 * 0.044715 * preact * preact)


def dft_table(count, order_count):
    lon_index = jnp.arange(count, dtype=jnp.int32)[:, None]
    order_index = jnp.arange(order_count, dtype=jnp.int32)[None, :]
    angles = (lon_index * order_index % count).astype(jnp.float32) * (2.0 * math.pi / count)
    factor = 1.0 / math.sqrt(count)
    return jnp.stack([jnp.cos(angles) * factor, -jnp.sin(angles) * factor]).astype(jnp.bfloat16)


def on_device(stream, cotangent, w_expand, w_reduce, legendre, quadrature, spectral_mix):
    lat_count = lax.axis_size("lat")
    lon_count = lax.axis_size("lon")
    rows_here = stream.shape[0]
    cols_here = stream.shape[1]
    channels = stream.shape[2]
    tokens_all = rows_here * cols_here * lat_count * lon_count
    tokens = stream.reshape(-1, channels)
    upstream = cotangent.reshape(-1, channels)
    preact = jnp.dot(tokens, w_expand, preferred_element_type=jnp.float32)
    active = gelu_value(preact).astype(jnp.bfloat16)
    through = lax.dot_general(
        upstream, w_reduce, (((1,), (1,)), ((), ())), preferred_element_type=jnp.float32
    )
    dpreact = (through * gelu_slope(preact)).astype(jnp.bfloat16)
    factor = 1.0 / math.sqrt(tokens_all)
    grad_in = (
        lax.dot_general(
            tokens, dpreact, (((0,), (0,)), ((), ())), preferred_element_type=jnp.float32
        )
        * factor
    )
    grad_out = (
        lax.dot_general(
            active, upstream, (((0,), (0,)), ((), ())), preferred_element_type=jnp.float32
        )
        * factor
    )
    grad_expand, grad_reduce = lax.psum((grad_in, grad_out), ("lat", "lon"))
    back_proj = lax.dot_general(
        dpreact, w_expand, (((1,), (1,)), ((), ())), preferred_element_type=jnp.float32
    )
    skip_grad = (
        (upstream.astype(jnp.float32) + back_proj)
        .astype(jnp.bfloat16)
        .reshape(rows_here, cols_here, channels)
    )
    columns = lax.all_to_all(skip_grad, "lon", split_axis=2, concat_axis=1, tiled=True)
    lon_total = columns.shape[1]
    order_count = lon_total // 2
    basis = dft_table(lon_total, order_count)
    fourier = jnp.einsum(
        "anc,knm->kmac", columns, basis, preferred_element_type=jnp.float32
    ).astype(jnp.bfloat16)
    spectrum = lax.all_to_all(
        lax.all_to_all(fourier, "lat", split_axis=1, concat_axis=2, tiled=True),
        "lon",
        split_axis=1,
        concat_axis=3,
        tiled=True,
    )
    by_order = jnp.einsum(
        "kmac,mal->kmlc", spectrum, legendre, preferred_element_type=jnp.float32
    ).astype(jnp.bfloat16)
    by_degree = lax.all_to_all(
        lax.all_to_all(by_order, "lat", split_axis=2, concat_axis=1, tiled=True),
        "lon",
        split_axis=2,
        concat_axis=1,
        tiled=True,
    )
    mixed_coef = jnp.einsum(
        "kmlc,ldc->kmld", by_degree, spectral_mix, preferred_element_type=jnp.float32
    ).astype(jnp.bfloat16)
    returned = lax.all_to_all(
        lax.all_to_all(mixed_coef, "lon", split_axis=1, concat_axis=2, tiled=True),
        "lat",
        split_axis=1,
        concat_axis=2,
        tiled=True,
    )
    summed = jnp.einsum("kmlc,mal->kmac", returned, legendre, preferred_element_type=jnp.float32)
    synthesis = (summed * quadrature[None, None, :, None]).astype(jnp.bfloat16)
    fourier_back = lax.all_to_all(
        lax.all_to_all(synthesis, "lon", split_axis=3, concat_axis=1, tiled=True),
        "lat",
        split_axis=2,
        concat_axis=1,
        tiled=True,
    )
    grid_back = jnp.einsum(
        "kmac,knm->anc", fourier_back, basis, preferred_element_type=jnp.float32
    ).astype(jnp.bfloat16)
    returned_grid = lax.all_to_all(grid_back, "lon", split_axis=1, concat_axis=2, tiled=True)
    grad_input = (skip_grad.astype(jnp.float32) + returned_grid.astype(jnp.float32)).astype(
        jnp.bfloat16
    )
    return (grad_input, grad_expand, grad_reduce)


MESH = pl.DeviceIdType.MESH


def greet(count, me, device_of):
    barrier = pltpu.get_barrier_semaphore()

    def hello(off, carry):
        pl.semaphore_signal(
            barrier, inc=1, device_id=device_of(lax.rem(me + off, count)), device_id_type=MESH
        )
        return carry

    lax.fori_loop(1, count, hello, 0)
    pl.semaphore_wait(barrier, count - 1)


def place_of(lon_only):
    lat_index = lax.axis_index("lat")
    lon_index = lax.axis_index("lon")
    lon_count = lax.axis_size("lon")
    if lon_only:
        return lon_index, lon_count, lambda j: (lat_index, j)
    count = lax.axis_size("lat") * lon_count
    return (
        lat_index * lon_count + lon_index,
        count,
        lambda j: (lax.div(j, lon_count), lax.rem(j, lon_count)),
    )


def exchange_body(lon_only, views, *refs):
    width = len(views)
    ins, outs = refs[:width], refs[width : 2 * width]
    send_sem, recv_sem, own_sem = refs[2 * width :]
    me, count, device_of = place_of(lon_only)
    greet(count, me, device_of)

    def remote(n, off, target, landing):
        return pltpu.make_async_remote_copy(
            src_ref=views[n][0](ins[n], target),
            dst_ref=views[n][1](outs[n], landing),
            send_sem=send_sem.at[n, off],
            recv_sem=recv_sem.at[n, off],
            device_id=device_of(target),
            device_id_type=MESH,
        )

    def launch(off, carry):
        for n in range(width):
            remote(n, off, lax.rem(me + off, count), me).start()
        return carry

    lax.fori_loop(1, count, launch, 0)
    own = [
        pltpu.make_async_copy(views[n][0](ins[n], me), views[n][1](outs[n], me), own_sem.at[n])
        for n in range(width)
    ]
    for copy in own:
        copy.start()
    for copy in own:
        copy.wait()

    def finish(off, carry):
        for n in range(width):
            copy = remote(n, off, lax.rem(me + off, count), lax.rem(me + count - off, count))
            copy.wait_send()
            copy.wait_recv()
        return carry

    lax.fori_loop(1, count, finish, 0)


def exchange(arrays, shapes, views, lon_only, collective_id):
    count = lax.axis_size("lon") * (1 if lon_only else lax.axis_size("lat"))
    width = len(arrays)
    return pl.pallas_call(
        functools.partial(exchange_body, lon_only, views),
        out_shape=[jax.ShapeDtypeStruct(s, a.dtype) for s, a in zip(shapes, arrays)],
        in_specs=[pl.BlockSpec(memory_space=pl.ANY)] * width,
        out_specs=[pl.BlockSpec(memory_space=pl.ANY)] * width,
        scratch_shapes=[
            pltpu.SemaphoreType.DMA((width, count)),
            pltpu.SemaphoreType.DMA((width, count)),
            pltpu.SemaphoreType.DMA((width,)),
        ],
        compiler_params=pltpu.CompilerParams(collective_id=collective_id, has_side_effects=True),
    )(*arrays)


CUTS = 2


def mix_body(
    b_ref, mix_ref, g_ref, w_ref, gall_ref, got, made,
    fs_sem, fr_sem, bs_sem, br_sem, gs_sem, gr_sem, own_sem,
):
    me, count, device_of = place_of(False)
    depth = got.shape[1]
    part = depth // CUTS
    orders, channels = got.shape[3], got.shape[4]
    greet(count, me, device_of)

    def forward(k, h, off, target, landing):
        return pltpu.make_async_remote_copy(
            src_ref=b_ref.at[k, target, pl.ds(h * part, part)],
            dst_ref=got.at[k, pl.ds(h * part, part), landing],
            send_sem=fs_sem.at[k * CUTS + h, off],
            recv_sem=fr_sem.at[k * CUTS + h, off],
            device_id=device_of(target),
            device_id_type=MESH,
        )

    def back(k, h, off, target, landing):
        return pltpu.make_async_remote_copy(
            src_ref=made.at[k, pl.ds(h * part, part), target],
            dst_ref=w_ref.at[k, landing, pl.ds(h * part, part)],
            send_sem=bs_sem.at[k * CUTS + h, off],
            recv_sem=br_sem.at[k * CUTS + h, off],
            device_id=device_of(target),
            device_id_type=MESH,
        )

    def gather(off, landing):
        return pltpu.make_async_remote_copy(
            src_ref=g_ref,
            dst_ref=gall_ref.at[landing],
            send_sem=gs_sem.at[off],
            recv_sem=gr_sem.at[off],
            device_id=device_of(lax.rem(me + off, count)),
            device_id_type=MESH,
        )

    def over(first, last, step):
        def run(at, carry):
            step(at)
            return carry

        lax.fori_loop(first, last, run, 0)

    chunks = [(k, h) for k in range(2) for h in range(CUTS)]
    for k, h in chunks:
        over(1, count - me, lambda off: forward(k, h, off, me + off, me).start())
    over(1, count, lambda off: gather(off, me).start())
    own = [
        pltpu.make_async_copy(b_ref.at[k, me], got.at[k, :, me], own_sem.at[k]) for k in range(2)
    ] + [pltpu.make_async_copy(g_ref, gall_ref.at[me], own_sem.at[2])]
    for copy in own:
        copy.start()
    for copy in own:
        copy.wait()
    for k, h in chunks:
        over(1, me + 1, lambda off: forward(k, h, off, me, me - off).wait_recv())

        def mix(l):
            rows = got[k, l].reshape(count * orders, channels)
            made[k, l] = (
                lax.dot_general(
                    rows, mix_ref[l], (((1,), (1,)), ((), ())), preferred_element_type=jnp.float32
                )
                .astype(jnp.bfloat16)
                .reshape(count, orders, channels)
            )

        over(h * part, (h + 1) * part, mix)
        over(1, me + 1, lambda off: back(k, h, off, me - off, me).start())
    own = [
        pltpu.make_async_copy(made.at[k, :, me], w_ref.at[k, me], own_sem.at[k]) for k in range(2)
    ]
    for copy in own:
        copy.start()
    for copy in own:
        copy.wait()
    for k, h in chunks:
        over(1, count - me, lambda off: forward(k, h, off, me + off, me).wait_send())
        over(1, me + 1, lambda off: back(k, h, off, me - off, me).wait_send())
        over(1, count - me, lambda off: back(k, h, off, me, me + off).wait_recv())

    def gathered(off):
        copy = gather(off, lax.rem(me + count - off, count))
        copy.wait_send()
        copy.wait_recv()

    over(1, count, gathered)


def mix_exchange(by_order, spectral_mix, reduced, collective_id):
    _, count, depth, orders, channels = by_order.shape
    sems = pltpu.SemaphoreType.DMA((2 * CUTS, count))
    return pl.pallas_call(
        mix_body,
        out_shape=[
            jax.ShapeDtypeStruct(by_order.shape, jnp.bfloat16),
            jax.ShapeDtypeStruct((count,) + reduced.shape, reduced.dtype),
        ],
        in_specs=[
            pl.BlockSpec(memory_space=pl.ANY),
            pl.BlockSpec(memory_space=pltpu.VMEM),
            pl.BlockSpec(memory_space=pl.ANY),
        ],
        out_specs=[pl.BlockSpec(memory_space=pl.ANY)] * 2,
        scratch_shapes=[
            pltpu.VMEM((2, depth, count, orders, channels), jnp.bfloat16),
            pltpu.VMEM((2, depth, count, orders, channels), jnp.bfloat16),
            sems,
            sems,
            sems,
            sems,
            pltpu.SemaphoreType.DMA((count,)),
            pltpu.SemaphoreType.DMA((count,)),
            pltpu.SemaphoreType.DMA((3,)),
        ],
        compiler_params=pltpu.CompilerParams(
            collective_id=collective_id, has_side_effects=True, vmem_limit_bytes=40 * 2**20
        ),
    )(by_order, spectral_mix, reduced)


def direct(stream, cotangent, w_expand, w_reduce, legendre, quadrature, spectral_mix):
    lat_count = lax.axis_size("lat")
    lon_count = lax.axis_size("lon")
    count = lat_count * lon_count
    me = lax.axis_index("lat") * lon_count + lax.axis_index("lon")
    rows_here, cols_here, channels = stream.shape
    hidden = w_expand.shape[1]
    lon_total = cols_here * lon_count
    rows_own = rows_here // lon_count
    orders, rows_all, degrees = legendre.shape
    depth = degrees // count
    tokens = stream.reshape(-1, channels)
    upstream = cotangent.reshape(-1, channels)
    preact = jnp.dot(tokens, w_expand, preferred_element_type=jnp.float32)
    active = gelu_value(preact).astype(jnp.bfloat16)
    through = lax.dot_general(
        upstream, w_reduce, (((1,), (1,)), ((), ())), preferred_element_type=jnp.float32
    )
    dpreact = (through * gelu_slope(preact)).astype(jnp.bfloat16)
    back_proj = lax.dot_general(
        dpreact, w_expand, (((1,), (1,)), ((), ())), preferred_element_type=jnp.float32
    )
    skip_grad = (
        (upstream.astype(jnp.float32) + back_proj)
        .astype(jnp.bfloat16)
        .reshape(rows_here, cols_here, channels)
    )
    grad_in = lax.dot_general(
        tokens, dpreact, (((0,), (0,)), ((), ())), preferred_element_type=jnp.float32
    )
    grad_out = lax.dot_general(
        upstream, active, (((0,), (0,)), ((), ())), preferred_element_type=jnp.float32
    )
    grads = jnp.concatenate(
        [grad_in.reshape(count, -1, hidden), grad_out.reshape(count, -1, hidden)], axis=1
    )

    (rows,) = exchange(
        [skip_grad],
        [(rows_own, lon_total, channels)],
        [
            (
                lambda ref, j: ref.at[pl.ds(j * rows_own, rows_own)],
                lambda ref, j: ref.at[:, pl.ds(j * cols_here, cols_here)],
            )
        ],
        True,
        0,
    )
    basis = dft_table(lon_total, lon_total // 2)
    fourier = lax.dot_general(
        jnp.transpose(basis, (2, 0, 1)).reshape(lon_total, lon_total),
        rows,
        (((1,), (1,)), ((), ())),
        preferred_element_type=jnp.float32,
    ).astype(jnp.bfloat16)
    lead = lambda ref, j: ref.at[j]
    blocks, terms = exchange(
        [fourier.reshape(count, 2 * orders, rows_own * channels), grads],
        [(count, 2 * orders, rows_own * channels), grads.shape],
        [(lead, lead), (lead, lead)],
        False,
        1,
    )
    reduced = jnp.sum(terms, axis=0) * (1.0 / math.sqrt(rows_here * cols_here * count))
    spectrum = jnp.transpose(
        blocks.reshape(count, orders, 2, rows_own, channels), (2, 1, 0, 3, 4)
    ).reshape(2, orders, rows_all, channels)
    by_order = (
        jnp.einsum("mal,kmac->klmc", legendre, spectrum, preferred_element_type=jnp.float32)
        .astype(jnp.bfloat16)
        .reshape(2, count, depth, orders, channels)
    )
    mixed, gathered = mix_exchange(by_order, spectral_mix, reduced, 2)
    arrived = lax.broadcasted_iota(jnp.int32, mixed.shape, 1) >= me
    mixed = jnp.where(arrived, mixed, jnp.zeros_like(mixed)).reshape(2, degrees, orders, channels)
    summed = jnp.einsum("klmc,mal->mkac", mixed, legendre, preferred_element_type=jnp.float32)
    synthesis = (summed * quadrature[None, None, :, None]).astype(jnp.bfloat16)
    synthesis = jnp.transpose(
        synthesis.reshape(2 * orders, count, rows_own, channels), (1, 0, 2, 3)
    ).reshape(count, 2 * orders, rows_own * channels)
    (waves,) = exchange([synthesis], [synthesis.shape], [(lead, lead)], False, 3)
    waves = waves.reshape(lon_total, rows_own, channels)
    grid_back = lax.dot_general(
        waves,
        jnp.transpose(basis, (2, 0, 1)).reshape(lon_total, lon_total),
        (((0,), (0,)), ((), ())),
        preferred_element_type=jnp.float32,
    ).astype(jnp.bfloat16)
    grid_back = jnp.transpose(grid_back, (0, 2, 1))
    (returned_grid,) = exchange(
        [grid_back],
        [stream.shape],
        [
            (
                lambda ref, j: ref.at[:, pl.ds(j * cols_here, cols_here)],
                lambda ref, j: ref.at[pl.ds(j * rows_own, rows_own)],
            )
        ],
        True,
        4,
    )
    grad_input = (skip_grad.astype(jnp.float32) + returned_grid.astype(jnp.float32)).astype(
        jnp.bfloat16
    )
    half = gathered.shape[1] // 2
    grad_expand = gathered[:, :half].reshape(channels, hidden)
    grad_reduce = gathered[:, half:].reshape(channels, hidden).T
    return (grad_input, grad_expand, grad_reduce)


def on_either(stream, cotangent, w_expand, w_reduce, legendre, quadrature, spectral_mix):
    count = lax.axis_size("lat") * lax.axis_size("lon")
    whole_tiles = (
        legendre.shape[0] % 16 == 0
        and spectral_mix.shape[0] % CUTS == 0
        and stream.shape[0] % lax.axis_size("lon") == 0
        and stream.shape[1] % 16 == 0
        and w_expand.shape[0] % (8 * count) == 0
    )
    chosen = direct if whole_tiles else on_device
    return chosen(stream, cotangent, w_expand, w_reduce, legendre, quadrature, spectral_mix)


def solution(mesh):
    placed = (
        P("lat", "lon", None),
        P("lat", "lon", None),
        P(),
        P(),
        P(("lat", "lon"), None, None),
        P(),
        P(("lat", "lon"), None, None),
    )
    return jax.shard_map(
        on_either,
        mesh=mesh,
        in_specs=placed,
        out_specs=(P("lat", "lon", None), P(), P()),
        check_vma=False,
    )
```

```python
import functools
import math

import jax
import jax.numpy as jnp
import numpy as np
from jax import lax
from jax.experimental import pallas as pl
from jax.experimental.pallas import tpu as pltpu
from jax.sharding import PartitionSpec as P


def gelu_value(preact):
    inside = 0.7978845608028654 * (preact + 0.044715 * preact * preact * preact)
    return 0.5 * preact * (1.0 + jnp.tanh(inside))


def gelu_slope(preact):
    inside = 0.7978845608028654 * (preact + 0.044715 * preact * preact * preact)
    tanh_val = jnp.tanh(inside)
    return 0.5 * (1.0 + tanh_val) + 0.5 * preact * (
        1.0 - tanh_val * tanh_val
    ) * 0.7978845608028654 * (1.0 + 3.0 * 0.044715 * preact * preact)


def dft_table(count, order_count):
    lon_index = jnp.arange(count, dtype=jnp.int32)[:, None]
    order_index = jnp.arange(order_count, dtype=jnp.int32)[None, :]
    angles = (lon_index * order_index % count).astype(jnp.float32) * (2.0 * math.pi / count)
    factor = 1.0 / math.sqrt(count)
    return jnp.stack([jnp.cos(angles) * factor, -jnp.sin(angles) * factor]).astype(jnp.bfloat16)


def on_device(stream, cotangent, w_expand, w_reduce, legendre, quadrature, spectral_mix):
    lat_count = lax.axis_size("lat")
    lon_count = lax.axis_size("lon")
    rows_here = stream.shape[0]
    cols_here = stream.shape[1]
    channels = stream.shape[2]
    tokens_all = rows_here * cols_here * lat_count * lon_count
    tokens = stream.reshape(-1, channels)
    upstream = cotangent.reshape(-1, channels)
    preact = jnp.dot(tokens, w_expand, preferred_element_type=jnp.float32)
    active = gelu_value(preact).astype(jnp.bfloat16)
    through = lax.dot_general(
        upstream, w_reduce, (((1,), (1,)), ((), ())), preferred_element_type=jnp.float32
    )
    dpreact = (through * gelu_slope(preact)).astype(jnp.bfloat16)
    factor = 1.0 / math.sqrt(tokens_all)
    grad_in = (
        lax.dot_general(
            tokens, dpreact, (((0,), (0,)), ((), ())), preferred_element_type=jnp.float32
        )
        * factor
    )
    grad_out = (
        lax.dot_general(
            active, upstream, (((0,), (0,)), ((), ())), preferred_element_type=jnp.float32
        )
        * factor
    )
    grad_expand, grad_reduce = lax.psum((grad_in, grad_out), ("lat", "lon"))
    back_proj = lax.dot_general(
        dpreact, w_expand, (((1,), (1,)), ((), ())), preferred_element_type=jnp.float32
    )
    skip_grad = (
        (upstream.astype(jnp.float32) + back_proj)
        .astype(jnp.bfloat16)
        .reshape(rows_here, cols_here, channels)
    )
    columns = lax.all_to_all(skip_grad, "lon", split_axis=2, concat_axis=1, tiled=True)
    lon_total = columns.shape[1]
    order_count = lon_total // 2
    basis = dft_table(lon_total, order_count)
    fourier = jnp.einsum(
        "anc,knm->kmac", columns, basis, preferred_element_type=jnp.float32
    ).astype(jnp.bfloat16)
    spectrum = lax.all_to_all(
        lax.all_to_all(fourier, "lat", split_axis=1, concat_axis=2, tiled=True),
        "lon",
        split_axis=1,
        concat_axis=3,
        tiled=True,
    )
    by_order = jnp.einsum(
        "kmac,mal->kmlc", spectrum, legendre, preferred_element_type=jnp.float32
    ).astype(jnp.bfloat16)
    by_degree = lax.all_to_all(
        lax.all_to_all(by_order, "lat", split_axis=2, concat_axis=1, tiled=True),
        "lon",
        split_axis=2,
        concat_axis=1,
        tiled=True,
    )
    mixed_coef = jnp.einsum(
        "kmlc,ldc->kmld", by_degree, spectral_mix, preferred_element_type=jnp.float32
    ).astype(jnp.bfloat16)
    returned = lax.all_to_all(
        lax.all_to_all(mixed_coef, "lon", split_axis=1, concat_axis=2, tiled=True),
        "lat",
        split_axis=1,
        concat_axis=2,
        tiled=True,
    )
    summed = jnp.einsum("kmlc,mal->kmac", returned, legendre, preferred_element_type=jnp.float32)
    synthesis = (summed * quadrature[None, None, :, None]).astype(jnp.bfloat16)
    fourier_back = lax.all_to_all(
        lax.all_to_all(synthesis, "lon", split_axis=3, concat_axis=1, tiled=True),
        "lat",
        split_axis=2,
        concat_axis=1,
        tiled=True,
    )
    grid_back = jnp.einsum(
        "kmac,knm->anc", fourier_back, basis, preferred_element_type=jnp.float32
    ).astype(jnp.bfloat16)
    returned_grid = lax.all_to_all(grid_back, "lon", split_axis=1, concat_axis=2, tiled=True)
    grad_input = (skip_grad.astype(jnp.float32) + returned_grid.astype(jnp.float32)).astype(
        jnp.bfloat16
    )
    return (grad_input, grad_expand, grad_reduce)


MESH = pl.DeviceIdType.MESH


def greet(count, me, device_of):
    barrier = pltpu.get_barrier_semaphore()

    def hello(off, carry):
        pl.semaphore_signal(
            barrier, inc=1, device_id=device_of(lax.rem(me + off, count)), device_id_type=MESH
        )
        return carry

    lax.fori_loop(1, count, hello, 0)
    pl.semaphore_wait(barrier, count - 1)


def place_of(lon_only):
    lat_index = lax.axis_index("lat")
    lon_index = lax.axis_index("lon")
    lon_count = lax.axis_size("lon")
    if lon_only:
        return lon_index, lon_count, lambda j: (lat_index, j)
    count = lax.axis_size("lat") * lon_count
    return (
        lat_index * lon_count + lon_index,
        count,
        lambda j: (lax.div(j, lon_count), lax.rem(j, lon_count)),
    )


def exchange_body(lon_only, views, *refs):
    width = len(views)
    ins, outs = refs[:width], refs[width : 2 * width]
    send_sem, recv_sem, own_sem = refs[2 * width :]
    me, count, device_of = place_of(lon_only)
    greet(count, me, device_of)

    def remote(n, off, target, landing):
        return pltpu.make_async_remote_copy(
            src_ref=views[n][0](ins[n], target),
            dst_ref=views[n][1](outs[n], landing),
            send_sem=send_sem.at[n, off],
            recv_sem=recv_sem.at[n, off],
            device_id=device_of(target),
            device_id_type=MESH,
        )

    def launch(off, carry):
        for n in range(width):
            remote(n, off, lax.rem(me + off, count), me).start()
        return carry

    lax.fori_loop(1, count, launch, 0)
    own = [
        pltpu.make_async_copy(views[n][0](ins[n], me), views[n][1](outs[n], me), own_sem.at[n])
        for n in range(width)
    ]
    for copy in own:
        copy.start()
    for copy in own:
        copy.wait()

    def finish(off, carry):
        for n in range(width):
            copy = remote(n, off, lax.rem(me + off, count), lax.rem(me + count - off, count))
            copy.wait_send()
            copy.wait_recv()
        return carry

    lax.fori_loop(1, count, finish, 0)


def exchange(arrays, shapes, views, lon_only, collective_id):
    count = lax.axis_size("lon") * (1 if lon_only else lax.axis_size("lat"))
    width = len(arrays)
    return pl.pallas_call(
        functools.partial(exchange_body, lon_only, views),
        out_shape=[jax.ShapeDtypeStruct(s, a.dtype) for s, a in zip(shapes, arrays)],
        in_specs=[pl.BlockSpec(memory_space=pl.ANY)] * width,
        out_specs=[pl.BlockSpec(memory_space=pl.ANY)] * width,
        scratch_shapes=[
            pltpu.SemaphoreType.DMA((width, count)),
            pltpu.SemaphoreType.DMA((width, count)),
            pltpu.SemaphoreType.DMA((width,)),
        ],
        compiler_params=pltpu.CompilerParams(collective_id=collective_id, has_side_effects=True),
    )(*arrays)


CUTS = 2


def mix_body(
    b_ref, mix_ref, g_ref, w_ref, gall_ref, got, made,
    fs_sem, fr_sem, bs_sem, br_sem, gs_sem, gr_sem, own_sem, blank, blank_sem,
):
    me, count, device_of = place_of(False)
    depth = got.shape[1]
    part = depth // CUTS
    orders, channels = got.shape[3], got.shape[4]
    greet(count, me, device_of)

    def forward(k, h, off, target, landing):
        return pltpu.make_async_remote_copy(
            src_ref=b_ref.at[k, target, pl.ds(h * part, part)],
            dst_ref=got.at[k, pl.ds(h * part, part), landing],
            send_sem=fs_sem.at[k * CUTS + h, off],
            recv_sem=fr_sem.at[k * CUTS + h, off],
            device_id=device_of(target),
            device_id_type=MESH,
        )

    def back(k, h, off, target, landing):
        return pltpu.make_async_remote_copy(
            src_ref=made.at[k, pl.ds(h * part, part), target],
            dst_ref=w_ref.at[k, landing, pl.ds(h * part, part)],
            send_sem=bs_sem.at[k * CUTS + h, off],
            recv_sem=br_sem.at[k * CUTS + h, off],
            device_id=device_of(target),
            device_id_type=MESH,
        )

    def gather(off, landing):
        return pltpu.make_async_remote_copy(
            src_ref=g_ref,
            dst_ref=gall_ref.at[landing],
            send_sem=gs_sem.at[off],
            recv_sem=gr_sem.at[off],
            device_id=device_of(lax.rem(me + off, count)),
            device_id_type=MESH,
        )

    def over(first, last, step):
        def run(at, carry):
            step(at)
            return carry

        lax.fori_loop(first, last, run, 0)

    chunks = [(k, h) for k in range(2) for h in range(CUTS)]
    for k, h in chunks:
        over(1, count - me, lambda off: forward(k, h, off, me + off, me).start())
    over(1, count, lambda off: gather(off, me).start())
    blank[...] = jnp.zeros_like(blank)

    def clear(k, j):
        return pltpu.make_async_copy(blank, w_ref.at[k, j], blank_sem.at[k, j])

    own = [
        pltpu.make_async_copy(b_ref.at[k, me], got.at[k, :, me], own_sem.at[k]) for k in range(2)
    ] + [pltpu.make_async_copy(g_ref, gall_ref.at[me], own_sem.at[2])]
    for copy in own:
        copy.start()
    for copy in own:
        copy.wait()
    for k in range(2):
        over(0, me, lambda j: clear(k, j).start())
    for k, h in chunks:
        over(1, me + 1, lambda off: forward(k, h, off, me, me - off).wait_recv())

        def mix(l):
            rows = got[k, l].reshape(count * orders, channels)
            made[k, l] = (
                lax.dot_general(
                    rows, mix_ref[l], (((1,), (1,)), ((), ())), preferred_element_type=jnp.float32
                )
                .astype(jnp.bfloat16)
                .reshape(count, orders, channels)
            )

        over(h * part, (h + 1) * part, mix)
        over(1, me + 1, lambda off: back(k, h, off, me - off, me).start())
    own = [
        pltpu.make_async_copy(made.at[k, :, me], w_ref.at[k, me], own_sem.at[k]) for k in range(2)
    ]
    for copy in own:
        copy.start()
    for copy in own:
        copy.wait()
    for k, h in chunks:
        over(1, count - me, lambda off: forward(k, h, off, me + off, me).wait_send())
        over(1, me + 1, lambda off: back(k, h, off, me - off, me).wait_send())
        over(1, count - me, lambda off: back(k, h, off, me, me + off).wait_recv())

    def gathered(off):
        copy = gather(off, lax.rem(me + count - off, count))
        copy.wait_send()
        copy.wait_recv()

    over(1, count, gathered)
    for k in range(2):
        over(0, me, lambda j: clear(k, j).wait())


def mix_exchange(by_order, spectral_mix, reduced, collective_id):
    _, count, depth, orders, channels = by_order.shape
    sems = pltpu.SemaphoreType.DMA((2 * CUTS, count))
    return pl.pallas_call(
        mix_body,
        out_shape=[
            jax.ShapeDtypeStruct(by_order.shape, jnp.bfloat16),
            jax.ShapeDtypeStruct((count,) + reduced.shape, reduced.dtype),
        ],
        in_specs=[
            pl.BlockSpec(memory_space=pl.ANY),
            pl.BlockSpec(memory_space=pltpu.VMEM),
            pl.BlockSpec(memory_space=pl.ANY),
        ],
        out_specs=[pl.BlockSpec(memory_space=pl.ANY)] * 2,
        scratch_shapes=[
            pltpu.VMEM((2, depth, count, orders, channels), jnp.bfloat16),
            pltpu.VMEM((2, depth, count, orders, channels), jnp.bfloat16),
            sems,
            sems,
            sems,
            sems,
            pltpu.SemaphoreType.DMA((count,)),
            pltpu.SemaphoreType.DMA((count,)),
            pltpu.SemaphoreType.DMA((3,)),
            pltpu.VMEM((depth, orders, channels), jnp.bfloat16),
            pltpu.SemaphoreType.DMA((2, count)),
        ],
        compiler_params=pltpu.CompilerParams(
            collective_id=collective_id, has_side_effects=True, vmem_limit_bytes=40 * 2**20
        ),
    )(by_order, spectral_mix, reduced)


def wave_rows(count):
    order_index = np.arange(count // 2, dtype=np.int64)[:, None]
    lon_index = np.arange(count, dtype=np.int64)[None, :]
    angles = (order_index * lon_index % count).astype(np.float32) * np.float32(
        2.0 * math.pi / count
    )
    factor = np.float32(1.0 / math.sqrt(count))
    table = np.stack([np.cos(angles) * factor, -np.sin(angles) * factor], axis=1)
    return table.reshape(count, count).astype(jnp.bfloat16)


def direct(stream, cotangent, w_expand, w_reduce, legendre, quadrature, spectral_mix):
    lat_count = lax.axis_size("lat")
    lon_count = lax.axis_size("lon")
    count = lat_count * lon_count
    rows_here, cols_here, channels = stream.shape
    hidden = w_expand.shape[1]
    lon_total = cols_here * lon_count
    rows_own = rows_here // lon_count
    orders, rows_all, degrees = legendre.shape
    depth = degrees // count
    tokens = stream.reshape(-1, channels)
    upstream = cotangent.reshape(-1, channels)
    preact = jnp.dot(tokens, w_expand, preferred_element_type=jnp.float32)
    active = gelu_value(preact).astype(jnp.bfloat16)
    through = lax.dot_general(
        upstream, w_reduce, (((1,), (1,)), ((), ())), preferred_element_type=jnp.float32
    )
    dpreact = (through * gelu_slope(preact)).astype(jnp.bfloat16)
    back_proj = lax.dot_general(
        dpreact, w_expand, (((1,), (1,)), ((), ())), preferred_element_type=jnp.float32
    )
    skip_grad = (
        (upstream.astype(jnp.float32) + back_proj)
        .astype(jnp.bfloat16)
        .reshape(rows_here, cols_here, channels)
    )
    grad_in = lax.dot_general(
        tokens, dpreact, (((0,), (0,)), ((), ())), preferred_element_type=jnp.float32
    )
    grad_out = lax.dot_general(
        upstream, active, (((0,), (0,)), ((), ())), preferred_element_type=jnp.float32
    )
    grads = jnp.concatenate(
        [grad_in.reshape(count, -1, hidden), grad_out.reshape(count, -1, hidden)], axis=1
    )

    (rows,) = exchange(
        [skip_grad],
        [(rows_own, lon_total, channels)],
        [
            (
                lambda ref, j: ref.at[pl.ds(j * rows_own, rows_own)],
                lambda ref, j: ref.at[:, pl.ds(j * cols_here, cols_here)],
            )
        ],
        True,
        0,
    )
    waves_of = jnp.asarray(wave_rows(lon_total))
    fourier = jnp.einsum(
        "pn,anc->apc", waves_of, rows, preferred_element_type=jnp.float32
    ).astype(jnp.bfloat16)
    lead = lambda ref, j: ref.at[j]
    by_orders = lambda ref, j: ref.at[:, pl.ds(j * 2 * orders, 2 * orders)]
    by_rows = lambda ref, j: ref.at[pl.ds(j * rows_own, rows_own)]
    blocks, terms = exchange(
        [fourier, grads.astype(jnp.bfloat16)],
        [(rows_all, 2 * orders, channels), grads.shape],
        [(by_orders, by_rows), (lead, lead)],
        False,
        1,
    )
    reduced = (
        jnp.sum(terms.astype(jnp.float32), axis=0)
        * (1.0 / math.sqrt(rows_here * cols_here * count))
    ).astype(jnp.bfloat16)
    spectrum = blocks.reshape(rows_all, orders, 2, channels)
    by_order = (
        jnp.einsum("mal,amkc->klmc", legendre, spectrum, preferred_element_type=jnp.float32)
        .astype(jnp.bfloat16)
        .reshape(2, count, depth, orders, channels)
    )
    mixed, gathered = mix_exchange(by_order, spectral_mix, reduced, 2)
    mixed = mixed.reshape(2, degrees, orders, channels)
    summed = jnp.einsum("klmc,mal->amkc", mixed, legendre, preferred_element_type=jnp.float32)
    synthesis = (
        (summed * quadrature[:, None, None, None])
        .astype(jnp.bfloat16)
        .reshape(rows_all, 2 * orders, channels)
    )
    (waves,) = exchange(
        [synthesis], [(rows_own, lon_total, channels)], [(by_rows, by_orders)], False, 3
    )
    grid_back = jnp.einsum(
        "apc,pn->anc", waves, waves_of, preferred_element_type=jnp.float32
    ).astype(jnp.bfloat16)
    (returned_grid,) = exchange(
        [grid_back],
        [stream.shape],
        [
            (
                lambda ref, j: ref.at[:, pl.ds(j * cols_here, cols_here)],
                lambda ref, j: ref.at[pl.ds(j * rows_own, rows_own)],
            )
        ],
        True,
        4,
    )
    grad_input = (skip_grad.astype(jnp.float32) + returned_grid.astype(jnp.float32)).astype(
        jnp.bfloat16
    )
    half = gathered.shape[1] // 2
    gathered = gathered.astype(jnp.float32)
    grad_expand = gathered[:, :half].reshape(channels, hidden)
    grad_reduce = gathered[:, half:].reshape(channels, hidden).T
    return (grad_input, grad_expand, grad_reduce)


def on_either(stream, cotangent, w_expand, w_reduce, legendre, quadrature, spectral_mix):
    count = lax.axis_size("lat") * lax.axis_size("lon")
    whole_tiles = (
        legendre.shape[0] % 16 == 0
        and spectral_mix.shape[0] % CUTS == 0
        and stream.shape[0] % lax.axis_size("lon") == 0
        and stream.shape[1] % 16 == 0
        and w_expand.shape[0] % (8 * count) == 0
    )
    chosen = direct if whole_tiles else on_device
    return chosen(stream, cotangent, w_expand, w_reduce, legendre, quadrature, spectral_mix)


def solution(mesh):
    placed = (
        P("lat", "lon", None),
        P("lat", "lon", None),
        P(),
        P(),
        P(("lat", "lon"), None, None),
        P(),
        P(("lat", "lon"), None, None),
    )
    return jax.shard_map(
        on_either,
        mesh=mesh,
        in_specs=placed,
        out_specs=(P("lat", "lon", None), P(), P()),
        check_vma=False,
    )
```

```python
import functools
import math

import jax
import jax.numpy as jnp
import numpy as np
from jax import lax
from jax.experimental import pallas as pl
from jax.experimental.pallas import tpu as pltpu
from jax.sharding import PartitionSpec as P


def gelu_value(preact):
    inside = 0.7978845608028654 * (preact + 0.044715 * preact * preact * preact)
    return 0.5 * preact * (1.0 + jnp.tanh(inside))


def gelu_slope(preact):
    inside = 0.7978845608028654 * (preact + 0.044715 * preact * preact * preact)
    tanh_val = jnp.tanh(inside)
    return 0.5 * (1.0 + tanh_val) + 0.5 * preact * (
        1.0 - tanh_val * tanh_val
    ) * 0.7978845608028654 * (1.0 + 3.0 * 0.044715 * preact * preact)


def dft_table(count, order_count):
    lon_index = jnp.arange(count, dtype=jnp.int32)[:, None]
    order_index = jnp.arange(order_count, dtype=jnp.int32)[None, :]
    angles = (lon_index * order_index % count).astype(jnp.float32) * (2.0 * math.pi / count)
    factor = 1.0 / math.sqrt(count)
    return jnp.stack([jnp.cos(angles) * factor, -jnp.sin(angles) * factor]).astype(jnp.bfloat16)


def on_device(stream, cotangent, w_expand, w_reduce, legendre, quadrature, spectral_mix):
    lat_count = lax.axis_size("lat")
    lon_count = lax.axis_size("lon")
    rows_here = stream.shape[0]
    cols_here = stream.shape[1]
    channels = stream.shape[2]
    tokens_all = rows_here * cols_here * lat_count * lon_count
    tokens = stream.reshape(-1, channels)
    upstream = cotangent.reshape(-1, channels)
    preact = jnp.dot(tokens, w_expand, preferred_element_type=jnp.float32)
    active = gelu_value(preact).astype(jnp.bfloat16)
    through = lax.dot_general(
        upstream, w_reduce, (((1,), (1,)), ((), ())), preferred_element_type=jnp.float32
    )
    dpreact = (through * gelu_slope(preact)).astype(jnp.bfloat16)
    factor = 1.0 / math.sqrt(tokens_all)
    grad_in = (
        lax.dot_general(
            tokens, dpreact, (((0,), (0,)), ((), ())), preferred_element_type=jnp.float32
        )
        * factor
    )
    grad_out = (
        lax.dot_general(
            active, upstream, (((0,), (0,)), ((), ())), preferred_element_type=jnp.float32
        )
        * factor
    )
    grad_expand, grad_reduce = lax.psum((grad_in, grad_out), ("lat", "lon"))
    back_proj = lax.dot_general(
        dpreact, w_expand, (((1,), (1,)), ((), ())), preferred_element_type=jnp.float32
    )
    skip_grad = (
        (upstream.astype(jnp.float32) + back_proj)
        .astype(jnp.bfloat16)
        .reshape(rows_here, cols_here, channels)
    )
    columns = lax.all_to_all(skip_grad, "lon", split_axis=2, concat_axis=1, tiled=True)
    lon_total = columns.shape[1]
    order_count = lon_total // 2
    basis = dft_table(lon_total, order_count)
    fourier = jnp.einsum(
        "anc,knm->kmac", columns, basis, preferred_element_type=jnp.float32
    ).astype(jnp.bfloat16)
    spectrum = lax.all_to_all(
        lax.all_to_all(fourier, "lat", split_axis=1, concat_axis=2, tiled=True),
        "lon",
        split_axis=1,
        concat_axis=3,
        tiled=True,
    )
    by_order = jnp.einsum(
        "kmac,mal->kmlc", spectrum, legendre, preferred_element_type=jnp.float32
    ).astype(jnp.bfloat16)
    by_degree = lax.all_to_all(
        lax.all_to_all(by_order, "lat", split_axis=2, concat_axis=1, tiled=True),
        "lon",
        split_axis=2,
        concat_axis=1,
        tiled=True,
    )
    mixed_coef = jnp.einsum(
        "kmlc,ldc->kmld", by_degree, spectral_mix, preferred_element_type=jnp.float32
    ).astype(jnp.bfloat16)
    returned = lax.all_to_all(
        lax.all_to_all(mixed_coef, "lon", split_axis=1, concat_axis=2, tiled=True),
        "lat",
        split_axis=1,
        concat_axis=2,
        tiled=True,
    )
    summed = jnp.einsum("kmlc,mal->kmac", returned, legendre, preferred_element_type=jnp.float32)
    synthesis = (summed * quadrature[None, None, :, None]).astype(jnp.bfloat16)
    fourier_back = lax.all_to_all(
        lax.all_to_all(synthesis, "lon", split_axis=3, concat_axis=1, tiled=True),
        "lat",
        split_axis=2,
        concat_axis=1,
        tiled=True,
    )
    grid_back = jnp.einsum(
        "kmac,knm->anc", fourier_back, basis, preferred_element_type=jnp.float32
    ).astype(jnp.bfloat16)
    returned_grid = lax.all_to_all(grid_back, "lon", split_axis=1, concat_axis=2, tiled=True)
    grad_input = (skip_grad.astype(jnp.float32) + returned_grid.astype(jnp.float32)).astype(
        jnp.bfloat16
    )
    return (grad_input, grad_expand, grad_reduce)


MESH = pl.DeviceIdType.MESH


def greet(count, me, device_of):
    barrier = pltpu.get_barrier_semaphore()

    def hello(off, carry):
        pl.semaphore_signal(
            barrier, inc=1, device_id=device_of(lax.rem(me + off, count)), device_id_type=MESH
        )
        return carry

    lax.fori_loop(1, count, hello, 0)
    pl.semaphore_wait(barrier, count - 1)


def place_of(lon_only):
    lat_index = lax.axis_index("lat")
    lon_index = lax.axis_index("lon")
    lon_count = lax.axis_size("lon")
    if lon_only:
        return lon_index, lon_count, lambda j: (lat_index, j)
    count = lax.axis_size("lat") * lon_count
    return (
        lat_index * lon_count + lon_index,
        count,
        lambda j: (lax.div(j, lon_count), lax.rem(j, lon_count)),
    )


def exchange_body(lon_only, views, *refs):
    width = len(views)
    ins, outs = refs[:width], refs[width : 2 * width]
    send_sem, recv_sem, own_sem = refs[2 * width :]
    me, count, device_of = place_of(lon_only)
    greet(count, me, device_of)

    def remote(n, off, target, landing):
        return pltpu.make_async_remote_copy(
            src_ref=views[n][0](ins[n], target),
            dst_ref=views[n][1](outs[n], landing),
            send_sem=send_sem.at[n, off],
            recv_sem=recv_sem.at[n, off],
            device_id=device_of(target),
            device_id_type=MESH,
        )

    def launch(off, carry):
        for n in range(width):
            remote(n, off, lax.rem(me + off, count), me).start()
        return carry

    lax.fori_loop(1, count, launch, 0)
    own = [
        pltpu.make_async_copy(views[n][0](ins[n], me), views[n][1](outs[n], me), own_sem.at[n])
        for n in range(width)
    ]
    for copy in own:
        copy.start()
    for copy in own:
        copy.wait()

    def finish(off, carry):
        for n in range(width):
            copy = remote(n, off, lax.rem(me + off, count), lax.rem(me + count - off, count))
            copy.wait_send()
            copy.wait_recv()
        return carry

    lax.fori_loop(1, count, finish, 0)


def exchange(arrays, shapes, views, lon_only, collective_id):
    count = lax.axis_size("lon") * (1 if lon_only else lax.axis_size("lat"))
    width = len(arrays)
    return pl.pallas_call(
        functools.partial(exchange_body, lon_only, views),
        out_shape=[jax.ShapeDtypeStruct(s, a.dtype) for s, a in zip(shapes, arrays)],
        in_specs=[pl.BlockSpec(memory_space=pl.ANY)] * width,
        out_specs=[pl.BlockSpec(memory_space=pl.ANY)] * width,
        scratch_shapes=[
            pltpu.SemaphoreType.DMA((width, count)),
            pltpu.SemaphoreType.DMA((width, count)),
            pltpu.SemaphoreType.DMA((width,)),
        ],
        compiler_params=pltpu.CompilerParams(collective_id=collective_id, has_side_effects=True),
    )(*arrays)


CUTS = 4


def mix_body(
    b_ref, mix_ref, g_ref, w_ref, gall_ref, got, made,
    fs_sem, fr_sem, bs_sem, br_sem, gs_sem, gr_sem, own_sem, blank, blank_sem,
):
    me, count, device_of = place_of(False)
    depth = got.shape[1]
    part = depth // CUTS
    orders, channels = got.shape[3], got.shape[4]
    greet(count, me, device_of)

    def forward(k, h, off, target, landing):
        return pltpu.make_async_remote_copy(
            src_ref=b_ref.at[k, target, pl.ds(h * part, part)],
            dst_ref=got.at[k, pl.ds(h * part, part), landing],
            send_sem=fs_sem.at[k * CUTS + h, off],
            recv_sem=fr_sem.at[k * CUTS + h, off],
            device_id=device_of(target),
            device_id_type=MESH,
        )

    def back(k, h, off, target, landing):
        return pltpu.make_async_remote_copy(
            src_ref=made.at[k, pl.ds(h * part, part), target],
            dst_ref=w_ref.at[k, landing, pl.ds(h * part, part)],
            send_sem=bs_sem.at[k * CUTS + h, off],
            recv_sem=br_sem.at[k * CUTS + h, off],
            device_id=device_of(target),
            device_id_type=MESH,
        )

    def gather(off, landing):
        return pltpu.make_async_remote_copy(
            src_ref=g_ref,
            dst_ref=gall_ref.at[landing],
            send_sem=gs_sem.at[off],
            recv_sem=gr_sem.at[off],
            device_id=device_of(lax.rem(me + off, count)),
            device_id_type=MESH,
        )

    def over(first, last, step):
        def run(at, carry):
            step(at)
            return carry

        lax.fori_loop(first, last, run, 0)

    chunks = [(k, h) for k in range(2) for h in range(CUTS)]
    for k, h in chunks:
        over(1, count - me, lambda off: forward(k, h, off, me + off, me).start())
    over(1, count, lambda off: gather(off, me).start())
    blank[...] = jnp.zeros_like(blank)

    def clear(k, j):
        return pltpu.make_async_copy(blank, w_ref.at[k, j], blank_sem.at[k, j])

    own = [
        pltpu.make_async_copy(b_ref.at[k, me], got.at[k, :, me], own_sem.at[k]) for k in range(2)
    ] + [pltpu.make_async_copy(g_ref, gall_ref.at[me], own_sem.at[2])]
    for copy in own:
        copy.start()
    for copy in own:
        copy.wait()
    for k in range(2):
        over(0, me, lambda j: clear(k, j).start())
    for k, h in chunks:
        over(1, me + 1, lambda off: forward(k, h, off, me, me - off).wait_recv())

        def mix(l):
            rows = got[k, l].reshape(count * orders, channels)
            made[k, l] = (
                lax.dot_general(
                    rows, mix_ref[l], (((1,), (1,)), ((), ())), preferred_element_type=jnp.float32
                )
                .astype(jnp.bfloat16)
                .reshape(count, orders, channels)
            )

        over(h * part, (h + 1) * part, mix)
        over(1, me + 1, lambda off: back(k, h, off, me - off, me).start())
    own = [
        pltpu.make_async_copy(made.at[k, :, me], w_ref.at[k, me], own_sem.at[k]) for k in range(2)
    ]
    for copy in own:
        copy.start()
    for copy in own:
        copy.wait()
    for k, h in chunks:
        over(1, count - me, lambda off: forward(k, h, off, me + off, me).wait_send())
        over(1, me + 1, lambda off: back(k, h, off, me - off, me).wait_send())
        over(1, count - me, lambda off: back(k, h, off, me, me + off).wait_recv())

    def gathered(off):
        copy = gather(off, lax.rem(me + count - off, count))
        copy.wait_send()
        copy.wait_recv()

    over(1, count, gathered)
    for k in range(2):
        over(0, me, lambda j: clear(k, j).wait())


def mix_exchange(by_order, spectral_mix, reduced, collective_id):
    _, count, depth, orders, channels = by_order.shape
    sems = pltpu.SemaphoreType.DMA((2 * CUTS, count))
    return pl.pallas_call(
        mix_body,
        out_shape=[
            jax.ShapeDtypeStruct(by_order.shape, jnp.bfloat16),
            jax.ShapeDtypeStruct((count,) + reduced.shape, reduced.dtype),
        ],
        in_specs=[
            pl.BlockSpec(memory_space=pl.ANY),
            pl.BlockSpec(memory_space=pltpu.VMEM),
            pl.BlockSpec(memory_space=pl.ANY),
        ],
        out_specs=[pl.BlockSpec(memory_space=pl.ANY)] * 2,
        scratch_shapes=[
            pltpu.VMEM((2, depth, count, orders, channels), jnp.bfloat16),
            pltpu.VMEM((2, depth, count, orders, channels), jnp.bfloat16),
            sems,
            sems,
            sems,
            sems,
            pltpu.SemaphoreType.DMA((count,)),
            pltpu.SemaphoreType.DMA((count,)),
            pltpu.SemaphoreType.DMA((3,)),
            pltpu.VMEM((depth, orders, channels), jnp.bfloat16),
            pltpu.SemaphoreType.DMA((2, count)),
        ],
        compiler_params=pltpu.CompilerParams(
            collective_id=collective_id, has_side_effects=True, vmem_limit_bytes=40 * 2**20
        ),
    )(by_order, spectral_mix, reduced)


def wave_rows(count):
    order_index = np.arange(count // 2, dtype=np.int64)[:, None]
    lon_index = np.arange(count, dtype=np.int64)[None, :]
    angles = (order_index * lon_index % count).astype(np.float32) * np.float32(
        2.0 * math.pi / count
    )
    factor = np.float32(1.0 / math.sqrt(count))
    table = np.stack([np.cos(angles) * factor, -np.sin(angles) * factor], axis=1)
    return table.reshape(count, count).astype(jnp.bfloat16)


def direct(stream, cotangent, w_expand, w_reduce, legendre, quadrature, spectral_mix):
    lat_count = lax.axis_size("lat")
    lon_count = lax.axis_size("lon")
    count = lat_count * lon_count
    rows_here, cols_here, channels = stream.shape
    hidden = w_expand.shape[1]
    lon_total = cols_here * lon_count
    rows_own = rows_here // lon_count
    orders, rows_all, degrees = legendre.shape
    depth = degrees // count
    tokens = stream.reshape(-1, channels)
    upstream = cotangent.reshape(-1, channels)
    preact = jnp.dot(tokens, w_expand, preferred_element_type=jnp.float32)
    active = gelu_value(preact).astype(jnp.bfloat16)
    through = lax.dot_general(
        upstream, w_reduce, (((1,), (1,)), ((), ())), preferred_element_type=jnp.float32
    )
    dpreact = (through * gelu_slope(preact)).astype(jnp.bfloat16)
    back_proj = lax.dot_general(
        dpreact, w_expand, (((1,), (1,)), ((), ())), preferred_element_type=jnp.float32
    )
    skip_grad = (
        (upstream.astype(jnp.float32) + back_proj)
        .astype(jnp.bfloat16)
        .reshape(rows_here, cols_here, channels)
    )
    grad_in = lax.dot_general(
        tokens, dpreact, (((0,), (0,)), ((), ())), preferred_element_type=jnp.float32
    )
    grad_out = lax.dot_general(
        upstream, active, (((0,), (0,)), ((), ())), preferred_element_type=jnp.float32
    )
    grads = jnp.concatenate(
        [grad_in.reshape(count, -1, hidden), grad_out.reshape(count, -1, hidden)], axis=1
    )

    (rows,) = exchange(
        [skip_grad],
        [(rows_own, lon_total, channels)],
        [
            (
                lambda ref, j: ref.at[pl.ds(j * rows_own, rows_own)],
                lambda ref, j: ref.at[:, pl.ds(j * cols_here, cols_here)],
            )
        ],
        True,
        0,
    )
    waves_of = jnp.asarray(wave_rows(lon_total))
    fourier = jnp.einsum(
        "pn,anc->apc", waves_of, rows, preferred_element_type=jnp.float32
    ).astype(jnp.bfloat16)
    lead = lambda ref, j: ref.at[j]
    by_orders = lambda ref, j: ref.at[:, pl.ds(j * 2 * orders, 2 * orders)]
    by_rows = lambda ref, j: ref.at[pl.ds(j * rows_own, rows_own)]
    blocks, terms = exchange(
        [fourier, grads.astype(jnp.bfloat16)],
        [(rows_all, 2 * orders, channels), grads.shape],
        [(by_orders, by_rows), (lead, lead)],
        False,
        1,
    )
    reduced = (
        jnp.sum(terms.astype(jnp.float32), axis=0)
        * (1.0 / math.sqrt(rows_here * cols_here * count))
    ).astype(jnp.bfloat16)
    spectrum = blocks.reshape(rows_all, orders, 2, channels)
    by_order = (
        jnp.einsum("mal,amkc->klmc", legendre, spectrum, preferred_element_type=jnp.float32)
        .astype(jnp.bfloat16)
        .reshape(2, count, depth, orders, channels)
    )
    mixed, gathered = mix_exchange(by_order, spectral_mix, reduced, 2)
    mixed = mixed.reshape(2, degrees, orders, channels)
    summed = jnp.einsum("klmc,mal->amkc", mixed, legendre, preferred_element_type=jnp.float32)
    synthesis = (
        (summed * quadrature[:, None, None, None])
        .astype(jnp.bfloat16)
        .reshape(rows_all, 2 * orders, channels)
    )
    (waves,) = exchange(
        [synthesis], [(rows_own, lon_total, channels)], [(by_rows, by_orders)], False, 3
    )
    grid_back = jnp.einsum(
        "apc,pn->anc", waves, waves_of, preferred_element_type=jnp.float32
    ).astype(jnp.bfloat16)
    (returned_grid,) = exchange(
        [grid_back],
        [stream.shape],
        [
            (
                lambda ref, j: ref.at[:, pl.ds(j * cols_here, cols_here)],
                lambda ref, j: ref.at[pl.ds(j * rows_own, rows_own)],
            )
        ],
        True,
        4,
    )
    grad_input = (skip_grad.astype(jnp.float32) + returned_grid.astype(jnp.float32)).astype(
        jnp.bfloat16
    )
    half = gathered.shape[1] // 2
    gathered = gathered.astype(jnp.float32)
    grad_expand = gathered[:, :half].reshape(channels, hidden)
    grad_reduce = gathered[:, half:].reshape(channels, hidden).T
    return (grad_input, grad_expand, grad_reduce)


def on_either(stream, cotangent, w_expand, w_reduce, legendre, quadrature, spectral_mix):
    count = lax.axis_size("lat") * lax.axis_size("lon")
    whole_tiles = (
        legendre.shape[0] % 16 == 0
        and spectral_mix.shape[0] % CUTS == 0
        and stream.shape[0] % lax.axis_size("lon") == 0
        and stream.shape[1] % 16 == 0
        and w_expand.shape[0] % (8 * count) == 0
    )
    chosen = direct if whole_tiles else on_device
    return chosen(stream, cotangent, w_expand, w_reduce, legendre, quadrature, spectral_mix)


def solution(mesh):
    placed = (
        P("lat", "lon", None),
        P("lat", "lon", None),
        P(),
        P(),
        P(("lat", "lon"), None, None),
        P(),
        P(("lat", "lon"), None, None),
    )
    return jax.shard_map(
        on_either,
        mesh=mesh,
        in_specs=placed,
        out_specs=(P("lat", "lon", None), P(), P()),
        check_vma=False,
    )
```
